256 devices in a mesh: shard: 16 (over x, z_hi, core), tp: 16 (over z_lo, y).
Axes of the slice: x: 4, y: 4, z: 8 (z_hi: 2, z_lo: 4; z = z_hi * 4 + z_lo), core: 2. Of those that a mesh axis runs over, the one named last changes fastest.
Arguments:
- master: float32 [8192, 4096], P('tp', 'shard'), may hold values from -0.56 to 0.56
- first_moment: float32 [8192, 4096], P('tp', 'shard'), may hold values from -0.5 to 0.5
- second_moment: float32 [8192, 4096], P('tp', 'shard'), may hold values from 0.01 to 0.2
- gradient: bfloat16 [8192, 4096], P('tp', 'shard'), may hold values from -4 to 4
- step_count: int32 [1], replicated, may hold values from 1 to 8
Outputs:
- new_master: float32 [8192, 4096], P('tp', 'shard')
- new_first: float32 [8192, 4096], P('tp', 'shard')
- new_second: float32 [8192, 4096], P('tp', 'shard')
- row_copy: bfloat16 [8192, 4096], P('tp')
- row_scales: bfloat16 [8192, 128], P('tp')
- col_copy: bfloat16 [16, 256, 8192], P(None, 'tp')
- col_scales: bfloat16 [16, 256, 256], P(None, 'tp')
The draws below stay inside these ranges and needn't reach their ends.
All inputs are finite; a program needn't handle non-finite values.
Results may differ from the reference program's by a relative error of at most 0.011.
Values may be sent and summed in bfloat16 or wider, within the bound.
A program may use at most 64 MiB of HBM per device.

```python
import math
import jax
import jax.numpy as jnp
from jax import lax

R = 8192
C = 4096
N_SHARD = 16


def draw_master(key, part):
    key = jax.random.fold_in(key, 11)
    keys = jax.random.split(key, 4)
    base = jax.random.truncated_normal(keys[0], -1.7320508, 1.7320508, (R, C), jnp.float32)
    lower, upper = (0.4, 4.0)
    row_scale = jnp.exp(jax.random.uniform(keys[1], (R, 1), jnp.float32, math.log(lower), math.log(upper)))
    col_scale = jnp.exp(jax.random.uniform(keys[2], (1, C), jnp.float32, math.log(lower), math.log(upper)))
    tiles = jax.random.randint(keys[3], (R // 32, C // 32), 0, 8)
    quiet = jnp.where(tiles == 0, 0.01, 1.0).astype(jnp.float32)
    quiet = jnp.repeat(jnp.repeat(quiet, 32, axis=0), 32, axis=1)
    return 0.02 * base * row_scale * col_scale * quiet


def level_of(stream_key, shape, shards, least, high):
    gain, own = 1.0, jax.random.fold_in(stream_key, 6)
    for axis_at, parts in shards:
        heights = jnp.exp(jax.random.uniform(jax.random.fold_in(own, axis_at), (parts,), jnp.float32, least / len(shards), high / len(shards)))
        gain = gain * jnp.repeat(heights, shape[axis_at] // parts).reshape([-1 if axis == axis_at else 1 for axis in range(len(shape))])
    return gain


def centred(key, shape, scale, most, shards=(), kind=jnp.bfloat16):
    gain = level_of(key, shape, shards, -0.22, 0.18) if shards else 1.0
    result = jax.random.normal(key, shape, jnp.float32) * scale * gain
    return jnp.minimum(jnp.maximum(result, -most), most).astype(kind)


def setup_inputs(seed: int = 0) -> dict:
    streams_of = jax.random.split(jax.random.key(seed), 6)
    master = draw_master(jax.random.fold_in(streams_of[5], 71), 0)
    first_moment = centred(streams_of[1], (R, C), 0.1, 0.5, ((0, 16), (1, 16)), jnp.float32)
    second_moment = jnp.clip(jnp.exp(math.log(0.2) - 2.9957323 * jax.random.uniform(streams_of[2], (R, C), jnp.float32) ** level_of(streams_of[2], (R, C), ((0, 16), (1, 16)), -0.2, 0.2)), 0.01, 0.2)
    gradient = centred(streams_of[3], (R, C), 1.0, 4.0, ((0, 16), (1, 16)))
    step_count = jax.random.randint(streams_of[4], (1,), 1, 9).astype(jnp.int32)
    return dict(master=master, first_moment=first_moment, second_moment=second_moment, gradient=gradient, step_count=step_count)


beta_one = 0.9
beta_two = 0.95
learn_rate = 0.02
epsilon = 1e-08
floor_value = 0.008
scale_unit = 64.0
block_size = 32

def quantize_blocks(values):
    dims = values.shape
    blocks = values.reshape(dims[:-1] + (dims[-1] // block_size, block_size))
    largest = lax.optimization_barrier(jnp.max(jnp.abs(blocks), axis=-1))
    scales = (scale_unit * jnp.maximum(largest, floor_value)).astype(jnp.bfloat16)
    payload = (scale_unit * blocks / scales.astype(jnp.float32)[..., None]).reshape(dims).astype(jnp.bfloat16)
    return (payload, scales)

def reference(master, first_moment, second_moment, gradient, step_count):
    steps_done = step_count[0].astype(jnp.float32)
    grad_full = gradient.astype(jnp.float32)
    new_first = beta_one * first_moment + (1.0 - beta_one) * grad_full
    new_second = beta_two * second_moment + (1.0 - beta_two) * grad_full * grad_full
    corr_one = 1.0 - jnp.power(beta_one, steps_done)
    corr_two = 1.0 - jnp.power(beta_two, steps_done)
    update = new_first / corr_one / (jnp.sqrt(new_second / corr_two) + epsilon)
    new_master = master - learn_rate * update
    row_copy, row_scales = quantize_blocks(new_master)
    col_payload, col_scale = quantize_blocks(new_master.T)
    col_copy = col_payload.reshape(N_SHARD, C // N_SHARD, R)
    col_scales = col_scale.reshape(N_SHARD, C // N_SHARD, R // block_size)
    return (new_master, new_first, new_second, row_copy, row_scales, col_copy, col_scales)
```

```python
import jax
import jax.numpy as jnp
from jax import lax
from jax.experimental import pallas as pl
from jax.experimental.pallas import tpu as pltpu
from jax.sharding import PartitionSpec as P

beta_one = 0.9
beta_two = 0.95
learn_rate = 0.02
epsilon = 1e-08
floor_value = 0.008
scale_unit = 64.0
block_size = 32

MESH = pl.DeviceIdType.MESH
BF16 = jnp.bfloat16
F32 = jnp.float32

ROWS, COLS, CHUNKS = 512, 256, 4
STEP = ROWS // CHUNKS
VMEM_LIMIT = 24 * 2**20

ROW_SCALES, COL_SCALES, ITEMS = 16, 17, 18

STEPS = (
    (0,), (1,), (2,), (3,), (0, 1), (8,), (2, 3), (4,), (5,), (9,), (15,), (10,), (14,), (8, 5), (11,), (13,),
    (4, 9), (6,), (10, 15), (7,), (12,), (14, 11), (6, 13), (12, 7),
)
WINDOW, ARRIVAL = 2, 3
SMALL = {7: (16,), 13: (17,), 11: (16, None), 17: (None, 17)}
Z_NEAR = (1, 7, 2, 6)
Z_LATER = {7: ((1, 7), (3, 5), ()), 10: ((2, 6), (), (2, 3)), 13: ((3, 5), (4,), ())}
COLUMNS_AT, ROW_SCALES_AT = 5, 20


def place():
    shard, tp = lax.axis_index("shard"), lax.axis_index("tp")
    return shard // 4, (shard // 2) % 2, shard % 2, tp // 4, tp % 4


def device(x, zh, core, zl, y):
    return (x * 4 + zh * 2 + core, zl * 4 + y)


def gather_kernel(
    step_ref, master, first, second, grad,
    new_master, new_first, new_second, row_out, row_scale_out, col_out, cs_out,
    master_v, first_v, second_v, grad_v,
    row_s, col_s, padded, flipped, flipped_s, held, held_s, sums, gathered_s, rs,
    load_sem, send_sem, left_sem, right_sem, opp_sem, sib_sem,
    zrow_sem, zrs_sem, y_sem, ys_sem, z_sem, zs_sem, right_sent, left_sent, row_sent, z_sent,
):
    x, zh, core, zl, y = place()
    z = zh * 4 + zl

    def along(dx=0, dy=0, dz=0, dcore=0):
        zz = (z + dz) % 8
        return device((x + dx) % 4, zz // 4, (core + dcore) % 2, zz % 4, (y + dy) % 4)

    partners = [(0, 0, dz, 0) for dz in (4, 3, 5, 2, 6, 1, 7)]
    partners += [(1, 0, 0, 0), (3, 0, 0, 0), (0, 2, 0, 0), (0, 1, 0, 0), (0, 3, 0, 0), (0, 0, 0, 1)]
    barrier = pltpu.get_barrier_semaphore()
    for partner in partners:
        pl.semaphore_signal(barrier, inc=1, device_id=along(*partner), device_id_type=MESH)

    loads = []
    for i in range(CHUNKS):
        part = pl.ds(i * STEP, STEP)
        loads.append([
            pltpu.make_async_copy(src.at[part], dst.at[part], load_sem.at[i, j])
            for j, (src, dst) in enumerate(
                ((master, master_v), (first, first_v), (second, second_v), (grad, grad_v))
            )
        ])
        for copy in loads[-1]:
            copy.start()

    def row_window(i, xx, half, cc):
        return row_out.at[xx, half, cc, pl.ds(i * STEP, STEP)]

    def view(item, dx):
        xx = (x + dx) % 4
        if item < 4:
            return row_window(item, xx, zh, core)
        if item < 8:
            return row_window(item - 4, xx, 1 - zh, core)
        if item < 16:
            source = (z + 16 - item) % 8
            lanes = pl.multiple_of((source % 4) * 4 * ROWS, 4 * ROWS)
            return col_out.at[xx, source // 4, core, :, pl.ds(lanes, 4 * ROWS)]
        return (rs if item == ROW_SCALES else cs_out).at[xx, :, core]

    def kind(item):
        return 0 if item < 8 else 1 if item < 16 else item - 14

    def remote(src, dst, sent, received, target):
        pltpu.make_async_remote_copy(
            src_ref=src, dst_ref=dst, send_sem=sent, recv_sem=received,
            device_id=target, device_id_type=MESH,
        ).start()

    def arrived(ref, sem):
        pltpu.make_async_copy(ref, ref, sem).wait()

    def move(item, dx, received, target):
        ref = view(item, dx)
        remote(ref, ref, send_sem.at[kind(item)], received, target)

    def to_sibling(item, dx):
        move(item, dx, sib_sem.at[kind(item)], along(dcore=1))

    def row_across(i):
        ref = row_window(i, x, zh, core)
        remote(ref, ref, row_sent.at[i], zrow_sem.at[i], along(dz=4))

    def z_across(dz):
        there = (z + dz) % 8 % 4
        remote(held.at[there], view(8, 0), z_sent.at[dz], z_sem.at[dz], along(dz=dz))

    waited = set()

    def arrive(side, item):
        if (side, item) not in waited:
            waited.add((side, item))
            dx, sem = {"left": (3, left_sem), "right": (1, right_sem), "opposite": (2, opp_sem)}[side]
            arrived(view(item, dx), sem.at[item])
            to_sibling(item, dx)

    def arrivals(group):
        if len(group) == 1:
            arrive("left", group[0])
            arrive("right", group[0])
            return
        for item in group:
            if item is not None:
                arrive("opposite", item)

    def send(group, right_sent, left_sent):
        if len(group) == 1:
            item = group[0]
            at_hand(item)
            ref = view(item, 0)
            remote(ref, ref, right_sent, left_sem.at[item], along(dx=1))
            remote(ref, ref, left_sent, right_sem.at[item], along(dx=3))
            to_sibling(item, 0)
            return
        item, other = group
        if item is not None:
            arrive("left", item)
            remote(view(item, 3), view(item, 3), right_sent, opp_sem.at[item], along(dx=1))
        if other is not None:
            arrive("right", other)
            remote(view(other, 1), view(other, 1), left_sent, opp_sem.at[other], along(dx=3))

    def at_hand(item):
        if 4 <= item < 8:
            arrived(row_window(item - 4, x, 1 - zh, core), zrow_sem.at[item - 4])
        elif 8 <= item < 16:
            arrived(view(item, 0), z_sem.at[item - 8])
        elif item == ROW_SCALES:
            arrived(rs.at[x, 1 - zh, core], zrs_sem.at[0])
        elif item == COL_SCALES:
            arrived(gathered_s, zs_sem.at[0])
            for half in range(2):
                pairs = gathered_s[half].astype(F32)
                low, high = pairs[0] + pairs[1], pairs[2] + pairs[3]
                cs_out[x, half, core] = jnp.concatenate([low, high], axis=1).astype(BF16)

    def sent(step):
        if ("sent", step) not in waited:
            waited.add(("sent", step))
            for sems in (right_sent, left_sent):
                arrived(row_out.at[0, 0, 0, :STEP], sems.at[step % WINDOW])

    def step_out(step):
        if step >= WINDOW:
            sent(step - WINDOW)
        send(STEPS[step], right_sent.at[step % WINDOW], left_sent.at[step % WINDOW])

    steps_done = jnp.full((8, 128), step_ref[0].astype(F32), F32)
    corr_one = (1.0 - jnp.power(beta_one, steps_done))[0:1, 0:1]
    corr_two = (1.0 - jnp.power(beta_two, steps_done))[0:1, 0:1]

    def scale(blocks):
        largest = jnp.max(jnp.abs(blocks), axis=1)
        scales = (scale_unit * jnp.maximum(largest, floor_value)).astype(BF16).astype(F32)
        return scales, blocks * (scale_unit / scales)[:, None, :]

    for i in range(CHUNKS):
        part = pl.ds(i * STEP, STEP)
        for copy in loads[i]:
            copy.wait()
        g = grad_v[part, :].astype(F32)
        nf = beta_one * first_v[part, :] + (1.0 - beta_one) * g
        nv = beta_two * second_v[part, :] + (1.0 - beta_two) * g * g
        update = nf / corr_one / (jnp.sqrt(nv / corr_two) + epsilon)
        m = master_v[part, :] - learn_rate * update
        new_first[part, :] = nf
        new_second[part, :] = nv
        new_master[part, :] = m

        scales, scaled = scale(m.T.reshape(COLS // block_size, block_size, STEP))
        row_s[:, part] = scales
        row_out[x, zh, core, part, :] = scaled.reshape(COLS, STEP).T.astype(BF16)
        if i == 0:
            pl.semaphore_wait(barrier, len(partners))
        if i < WINDOW:
            step_out(i)
            row_across(i)

        scales, scaled = scale(m.reshape(STEP // block_size, block_size, COLS))
        col_s[4 * i : 4 * i + 4, :] = scales
        flipped[:, part] = scaled.reshape(STEP, COLS).T.astype(BF16)

    values = flipped.reshape(4, 4, 16, ROWS)
    lanes = pl.ds(pl.multiple_of(y * ROWS, ROWS), ROWS)
    for dy in (2, 1, 3):
        there = (y + dy) % 4
        remote(values.at[:, there], held.at[:, :, lanes], send_sem.at[6], y_sem.at[0], along(dy=dy))
    pltpu.make_async_copy(values.at[:, y], held.at[:, :, lanes], y_sem.at[0]).start()

    own = row_s[...]
    rs[x, zh, core] = jnp.concatenate([own[:, :COLS], own[:, COLS:]], axis=0).astype(BF16)
    ref = rs.at[x, zh, core]
    remote(ref, ref, send_sem.at[5], zrs_sem.at[0], along(dz=4))

    padded[...] = jnp.zeros_like(padded)
    padded[pl.ds(pl.multiple_of(((zl * 4 + y) % 8) * 16, 16), 16), :] = col_s[...]
    flipped_s[...] = padded[...].T.astype(BF16)
    value_scales = flipped_s.reshape(4, 4, 16, 128)
    for dy in (2, 1, 3):
        there = (y + dy) % 4
        remote(value_scales.at[:, there], held_s.at[y], send_sem.at[7], ys_sem.at[0], along(dy=dy))
    pltpu.make_async_copy(value_scales.at[:, y], held_s.at[y], ys_sem.at[0]).start()

    for step in range(WINDOW, len(STEPS)):
        if step == COLUMNS_AT:
            arrived(held, y_sem.at[0])
            for i in range(WINDOW):
                arrived(row_window(i, x, zh, core), row_sent.at[i])
            for dz in Z_NEAR:
                z_across(dz)
            pltpu.make_async_copy(held.at[zl], view(8, 0), z_sem.at[0]).start()
        step_out(step)
        if step == COLUMNS_AT:
            arrived(held_s, ys_sem.at[0])
            parts = held_s[...].astype(F32)
            sums[...] = (parts[0] + parts[1] + parts[2] + parts[3]).astype(BF16)
            pltpu.make_async_copy(sums.at[zl], gathered_s.at[zh, zl], zs_sem.at[0]).start()
            for dz in range(1, 8):
                there = (z + dz) % 8 % 4
                remote(sums.at[there], gathered_s.at[zh, zl], send_sem.at[9], zs_sem.at[0], along(dz=dz))
        if step in Z_LATER:
            done, columns, rows = Z_LATER[step]
            for dz in done:
                arrived(view(8, 0), z_sent.at[dz])
            for dz in columns:
                z_across(dz)
            for i in rows:
                row_across(i)
        if step in SMALL:
            group = SMALL[step]
            sems = send_sem.at[max(i or 0 for i in group) - 14]
            send(group, sems, sems)
        if step >= ARRIVAL:
            arrivals(STEPS[step - ARRIVAL])
        if step - ARRIVAL in SMALL:
            arrivals(SMALL[step - ARRIVAL])
        if step == ROW_SCALES_AT + 1:
            arrived(rs.at[:, :, 0], sib_sem.at[2])
            scales = rs[...].astype(F32).reshape(16, 16, COLS)
            for half in range(2):
                one = scales[:, 8 * half : 8 * half + 8].reshape(128, COLS)
                row_scale_out[COLS * half : COLS * (half + 1), :] = one.T.astype(BF16)
    for step in range(len(STEPS) - ARRIVAL, len(STEPS)):
        arrivals(STEPS[step])

    arrived(cs_out.at[:, :, 0], sib_sem.at[3])
    arrived(row_out.at[:, :, 0], sib_sem.at[0])
    arrived(col_out.at[:, :, 0], sib_sem.at[1])
    arrived(flipped.at[: 3 * 64], send_sem.at[6])
    arrived(flipped_s.at[: 3 * 64], send_sem.at[7])
    arrived(rs.at[0, 0, 0], send_sem.at[5])
    arrived(row_out.at[0, 0, 0, :112, :128], send_sem.at[9])
    arrived(row_out.at[:, :, 0], send_sem.at[0])
    arrived(col_out.at[:, :, 0], send_sem.at[1])
    arrived(row_out.at[0, 0, 0, :224], send_sem.at[2])
    arrived(row_out.at[0, 0, 0, :224], send_sem.at[3])
    for i in range(WINDOW, CHUNKS):
        arrived(row_window(i, x, zh, core), row_sent.at[i])
    arrived(view(8, 0), z_sent.at[4])
    for step in range(len(STEPS)):
        sent(step)


def write_kernel(*refs):
    half = len(refs) // 2
    sems = refs[-1]
    pairs = []
    for src, dst in zip(refs[:half], refs[half : 2 * half]):
        if src.shape == dst.shape:
            pairs.append((src, dst))
            continue
        for s in range(16):
            pairs.append((src.at[s // 4, s // 2 % 2, s % 2], dst.at[:, pl.ds(s * COLS, COLS)]))
    copies = [pltpu.make_async_copy(src, dst, sems.at[i]) for i, (src, dst) in enumerate(pairs)]
    for copy in copies:
        copy.start()
    for copy in copies:
        copy.wait()


def body(master, first_moment, second_moment, gradient, step_count):
    block = (ROWS, COLS)
    shapes = [
        (block, F32), (block, F32), (block, F32),
        ((ROWS, 16 * COLS), BF16), ((ROWS, 128), BF16),
        ((4, 2, 2, 16, 16 * ROWS), BF16), ((4, 2, 2, 16, 256), BF16),
    ]
    held_shapes = shapes[:3] + [((4, 2, 2, ROWS, COLS), BF16)] + shapes[4:]
    vmem = pl.BlockSpec(memory_space=pltpu.VMEM)
    hbm = pl.BlockSpec(memory_space=pltpu.HBM)
    dma = pltpu.SemaphoreType.DMA
    place_in = pltpu.with_memory_space_constraint
    held = pl.pallas_call(
        gather_kernel,
        name="gather_copies",
        out_shape=[pltpu.VMEM(shape, dtype) for shape, dtype in held_shapes],
        in_specs=[pl.BlockSpec(memory_space=pltpu.SMEM)] + [hbm] * 4,
        out_specs=[vmem] * 7,
        scratch_shapes=[
            pltpu.VMEM(block, F32), pltpu.VMEM(block, F32), pltpu.VMEM(block, F32), pltpu.VMEM(block, BF16),
            pltpu.VMEM((8, ROWS), F32), pltpu.VMEM((16, COLS), F32), pltpu.VMEM((128, COLS), F32),
            pltpu.VMEM((COLS, ROWS), BF16), pltpu.VMEM((COLS, 128), BF16),
            pltpu.VMEM((4, 16, 4 * ROWS), BF16), pltpu.VMEM((4, 4, 16, 128), BF16),
            pltpu.VMEM((4, 16, 128), BF16), pltpu.VMEM((2, 4, 16, 128), BF16),
            pltpu.VMEM((4, 2, 2, 16, 256), BF16),
            dma((CHUNKS, 4)), dma((10,)), dma((ITEMS,)), dma((ITEMS,)), dma((ITEMS,)), dma((4,)),
            dma((4,)), dma((1,)), dma((1,)), dma((1,)), dma((8,)), dma((1,)),
            dma((WINDOW,)), dma((WINDOW,)), dma((CHUNKS,)), dma((8,)),
        ],
        compiler_params=pltpu.CompilerParams(
            collective_id=0, has_side_effects=True, vmem_limit_bytes=VMEM_LIMIT
        ),
    )(step_count, *(place_in(a, pltpu.HBM) for a in (master, first_moment, second_moment, gradient)))
    new_master, new_first, new_second, row_copy, row_scales, col_copy, col_scales = pl.pallas_call(
        write_kernel,
        name="write_results",
        out_shape=[jax.ShapeDtypeStruct(shape, dtype) for shape, dtype in shapes],
        in_specs=[vmem] * 7,
        out_specs=[hbm] * 7,
        scratch_shapes=[dma((22,))],
        compiler_params=pltpu.CompilerParams(vmem_limit_bytes=VMEM_LIMIT),
    )(*(place_in(a, pltpu.VMEM) for a in held))
    return (
        new_master, new_first, new_second, row_copy, row_scales,
        col_copy.reshape(16, 16, 16 * ROWS), col_scales.reshape(16, 16, 256),
    )


def solution(mesh):
    blocks = P("tp", "shard")
    in_specs = (blocks, blocks, blocks, blocks, P())
    out_specs = (
        blocks, blocks, blocks, P("tp", None), P("tp", None), P(None, "tp", None), P(None, "tp", None),
    )
    return jax.shard_map(body, mesh=mesh, in_specs=in_specs, out_specs=out_specs, check_vma=False)
```

```python
import jax
import jax.numpy as jnp
from jax import lax
from jax.experimental import pallas as pl
from jax.experimental.pallas import tpu as pltpu
from jax.sharding import PartitionSpec as P

beta_one = 0.9
beta_two = 0.95
learn_rate = 0.02
epsilon = 1e-08
floor_value = 0.008
scale_unit = 64.0
block_size = 32

MESH = pl.DeviceIdType.MESH
BF16 = jnp.bfloat16
F32 = jnp.float32

ROWS, COLS, CHUNKS = 512, 256, 4
STEP = ROWS // CHUNKS
VMEM_LIMIT = 24 * 2**20

ROW_SCALES, COL_SCALES, ITEMS = 16, 17, 18

STEPS = (
    (0,), (1,), (2,), (3,), (0, 1), (8,), (2, 3), (4,), (5,), (9,), (15,), (10,), (14,), (8, 5), (11,), (13,),
    (4, 9), (12,), (10, 15), (6,), (7,), (14, 11), (12, 13), (6, 7),
)
WINDOW, ARRIVAL = 3, 4
SMALL = {7: (16,), 13: (17,), 11: (16, None), 17: (None, 17)}
Z_NEAR = (1, 7, 2, 6)
Z_LATER = {6: ((1, 7), (3, 5), ()), 9: ((2, 6), (4,), ()), 12: ((3, 5), (), (2, 3))}
COLUMNS_AT, ROW_SCALES_AT = 5, 20


def place():
    shard, tp = lax.axis_index("shard"), lax.axis_index("tp")
    return shard // 4, (shard // 2) % 2, shard % 2, tp // 4, tp % 4


def device(x, zh, core, zl, y):
    return (x * 4 + zh * 2 + core, zl * 4 + y)


def gather_kernel(
    step_ref, master, first, second, grad,
    new_master, new_first, new_second, row_out, row_scale_out, col_out, cs_out,
    master_v, first_v, second_v, grad_v,
    row_s, col_s, padded, flipped, flipped_s, held, held_s, sums, gathered_s, rs,
    load_sem, send_sem, left_sem, right_sem, opp_sem, sib_sem,
    zrow_sem, zrs_sem, y_sem, ys_sem, z_sem, zs_sem, right_sent, left_sent, row_sent, z_sent,
):
    x, zh, core, zl, y = place()
    z = zh * 4 + zl

    def along(dx=0, dy=0, dz=0, dcore=0):
        zz = (z + dz) % 8
        return device((x + dx) % 4, zz // 4, (core + dcore) % 2, zz % 4, (y + dy) % 4)

    partners = [(0, 0, dz, 0) for dz in (4, 3, 5, 2, 6, 1, 7)]
    partners += [(1, 0, 0, 0), (3, 0, 0, 0), (0, 2, 0, 0), (0, 1, 0, 0), (0, 3, 0, 0), (0, 0, 0, 1)]
    barrier = pltpu.get_barrier_semaphore()
    for partner in partners:
        pl.semaphore_signal(barrier, inc=1, device_id=along(*partner), device_id_type=MESH)

    loads = []
    for i in range(CHUNKS):
        part = pl.ds(i * STEP, STEP)
        loads.append([
            pltpu.make_async_copy(src.at[part], dst.at[part], load_sem.at[i, j])
            for j, (src, dst) in enumerate(
                ((master, master_v), (first, first_v), (second, second_v), (grad, grad_v))
            )
        ])
        for copy in loads[-1]:
            copy.start()

    def row_window(i, xx, half, cc):
        return row_out.at[xx, half, cc, pl.ds(i * STEP, STEP)]

    def view(item, dx):
        xx = (x + dx) % 4
        if item < 4:
            return row_window(item, xx, zh, core)
        if item < 8:
            return row_window(item - 4, xx, 1 - zh, core)
        if item < 16:
            source = (z + 16 - item) % 8
            lanes = pl.multiple_of((source % 4) * 4 * ROWS, 4 * ROWS)
            return col_out.at[xx, source // 4, core, :, pl.ds(lanes, 4 * ROWS)]
        return (rs if item == ROW_SCALES else cs_out).at[xx, :, core]

    def kind(item):
        return 0 if item < 8 else 1 if item < 16 else item - 14

    def remote(src, dst, sent, received, target):
        pltpu.make_async_remote_copy(
            src_ref=src, dst_ref=dst, send_sem=sent, recv_sem=received,
            device_id=target, device_id_type=MESH,
        ).start()

    def arrived(ref, sem):
        pltpu.make_async_copy(ref, ref, sem).wait()

    def move(item, dx, received, target):
        ref = view(item, dx)
        remote(ref, ref, send_sem.at[kind(item)], received, target)

    def to_sibling(item, dx):
        move(item, dx, sib_sem.at[kind(item)], along(dcore=1))

    def row_across(i):
        ref = row_window(i, x, zh, core)
        remote(ref, ref, row_sent.at[i], zrow_sem.at[i], along(dz=4))

    def z_across(dz):
        there = (z + dz) % 8 % 4
        remote(held.at[there], view(8, 0), z_sent.at[dz], z_sem.at[dz], along(dz=dz))

    waited = set()

    def arrive(side, item):
        if (side, item) not in waited:
            waited.add((side, item))
            dx, sem = {"left": (3, left_sem), "right": (1, right_sem), "opposite": (2, opp_sem)}[side]
            arrived(view(item, dx), sem.at[item])
            to_sibling(item, dx)

    def arrivals(group):
        if len(group) == 1:
            arrive("left", group[0])
            arrive("right", group[0])
            return
        for item in group:
            if item is not None:
                arrive("opposite", item)

    def send(group, right_sent, left_sent):
        if len(group) == 1:
            item = group[0]
            at_hand(item)
            ref = view(item, 0)
            remote(ref, ref, right_sent, left_sem.at[item], along(dx=1))
            remote(ref, ref, left_sent, right_sem.at[item], along(dx=3))
            to_sibling(item, 0)
            return
        item, other = group
        if item is not None:
            arrive("left", item)
            remote(view(item, 3), view(item, 3), right_sent, opp_sem.at[item], along(dx=1))
        if other is not None:
            arrive("right", other)
            remote(view(other, 1), view(other, 1), left_sent, opp_sem.at[other], along(dx=3))

    def at_hand(item):
        if 4 <= item < 8:
            arrived(row_window(item - 4, x, 1 - zh, core), zrow_sem.at[item - 4])
        elif 8 <= item < 16:
            arrived(view(item, 0), z_sem.at[item - 8])
        elif item == ROW_SCALES:
            arrived(rs.at[x, 1 - zh, core], zrs_sem.at[0])
        elif item == COL_SCALES:
            arrived(gathered_s, zs_sem.at[0])
            for half in range(2):
                pairs = gathered_s[half].astype(F32)
                low, high = pairs[0] + pairs[1], pairs[2] + pairs[3]
                cs_out[x, half, core] = jnp.concatenate([low, high], axis=1).astype(BF16)

    def sent(step):
        if ("sent", step) not in waited:
            waited.add(("sent", step))
            for sems in (right_sent, left_sent):
                arrived(row_out.at[0, 0, 0, :STEP], sems.at[step % WINDOW])

    def step_out(step):
        if step >= WINDOW:
            sent(step - WINDOW)
        send(STEPS[step], right_sent.at[step % WINDOW], left_sent.at[step % WINDOW])

    steps_done = jnp.full((8, 128), step_ref[0].astype(F32), F32)
    corr_one = (1.0 - jnp.power(beta_one, steps_done))[0:1, 0:1]
    corr_two = (1.0 - jnp.power(beta_two, steps_done))[0:1, 0:1]

    def scale(blocks):
        largest = jnp.max(jnp.abs(blocks), axis=1)
        scales = (scale_unit * jnp.maximum(largest, floor_value)).astype(BF16).astype(F32)
        return scales, blocks * (scale_unit / scales)[:, None, :]

    values = flipped.reshape(4, 4, 16, ROWS)

    def y_across(half):
        here = pl.ds(half * COLS, COLS)
        lanes = pl.ds(pl.multiple_of(y * ROWS + half * COLS, COLS), COLS)
        for dy in (2, 1, 3):
            there = (y + dy) % 4
            remote(values.at[:, there, :, here], held.at[:, :, lanes], send_sem.at[6], y_sem.at[0], along(dy=dy))
        pltpu.make_async_copy(values.at[:, y, :, here], held.at[:, :, lanes], y_sem.at[0]).start()

    for i in range(CHUNKS):
        part = pl.ds(i * STEP, STEP)
        for copy in loads[i]:
            copy.wait()
        g = grad_v[part, :].astype(F32)
        nf = beta_one * first_v[part, :] + (1.0 - beta_one) * g
        nv = beta_two * second_v[part, :] + (1.0 - beta_two) * g * g
        update = nf / corr_one / (jnp.sqrt(nv / corr_two) + epsilon)
        m = master_v[part, :] - learn_rate * update
        new_first[part, :] = nf
        new_second[part, :] = nv
        new_master[part, :] = m

        scales, scaled = scale(m.T.reshape(COLS // block_size, block_size, STEP))
        row_s[:, part] = scales
        row_out[x, zh, core, part, :] = scaled.reshape(COLS, STEP).T.astype(BF16)
        if i == 0:
            pl.semaphore_wait(barrier, len(partners))
        if i < WINDOW:
            step_out(i)
        if i < 2:
            row_across(i)

        scales, scaled = scale(m.reshape(STEP // block_size, block_size, COLS))
        col_s[4 * i : 4 * i + 4, :] = scales
        flipped[:, part] = scaled.reshape(STEP, COLS).T.astype(BF16)
        if i % 2 == 1:
            y_across(i // 2)

    own = row_s[...]
    rs[x, zh, core] = jnp.concatenate([own[:, :COLS], own[:, COLS:]], axis=0).astype(BF16)
    ref = rs.at[x, zh, core]
    remote(ref, ref, send_sem.at[5], zrs_sem.at[0], along(dz=4))

    padded[...] = jnp.zeros_like(padded)
    padded[pl.ds(pl.multiple_of(((zl * 4 + y) % 8) * 16, 16), 16), :] = col_s[...]
    flipped_s[...] = padded[...].T.astype(BF16)
    value_scales = flipped_s.reshape(4, 4, 16, 128)
    for dy in (2, 1, 3):
        there = (y + dy) % 4
        remote(value_scales.at[:, there], held_s.at[y], send_sem.at[7], ys_sem.at[0], along(dy=dy))
    pltpu.make_async_copy(value_scales.at[:, y], held_s.at[y], ys_sem.at[0]).start()

    for step in range(WINDOW, len(STEPS)):
        if step == COLUMNS_AT:
            arrived(held, y_sem.at[0])
            for dz in Z_NEAR:
                z_across(dz)
            pltpu.make_async_copy(held.at[zl], view(8, 0), z_sem.at[0]).start()
        step_out(step)
        if step == COLUMNS_AT:
            arrived(held_s, ys_sem.at[0])
            parts = held_s[...].astype(F32)
            sums[...] = (parts[0] + parts[1] + parts[2] + parts[3]).astype(BF16)
            pltpu.make_async_copy(sums.at[zl], gathered_s.at[zh, zl], zs_sem.at[0]).start()
            for dz in range(1, 8):
                there = (z + dz) % 8 % 4
                remote(sums.at[there], gathered_s.at[zh, zl], send_sem.at[9], zs_sem.at[0], along(dz=dz))
        if step in Z_LATER:
            done, columns, rows = Z_LATER[step]
            for dz in done:
                arrived(view(8, 0), z_sent.at[dz])
            for dz in columns:
                z_across(dz)
            for i in rows:
                row_across(i)
        if step in SMALL:
            group = SMALL[step]
            sems = send_sem.at[max(i or 0 for i in group) - 14]
            send(group, sems, sems)
        if step >= ARRIVAL:
            arrivals(STEPS[step - ARRIVAL])
        if step - ARRIVAL in SMALL:
            arrivals(SMALL[step - ARRIVAL])
        if step == ROW_SCALES_AT + 1:
            arrived(rs.at[:, :, 0], sib_sem.at[2])
            scales = rs[...].astype(F32).reshape(16, 16, COLS)
            for half in range(2):
                one = scales[:, 8 * half : 8 * half + 8].reshape(128, COLS)
                row_scale_out[COLS * half : COLS * (half + 1), :] = one.T.astype(BF16)
    for step in range(len(STEPS) - ARRIVAL, len(STEPS)):
        arrivals(STEPS[step])

    arrived(cs_out.at[:, :, 0], sib_sem.at[3])
    arrived(row_out.at[:, :, 0], sib_sem.at[0])
    arrived(col_out.at[:, :, 0], sib_sem.at[1])
    arrived(flipped.at[: 3 * 64], send_sem.at[6])
    arrived(flipped_s.at[: 3 * 64], send_sem.at[7])
    arrived(rs.at[0, 0, 0], send_sem.at[5])
    arrived(row_out.at[0, 0, 0, :112, :128], send_sem.at[9])
    arrived(row_out.at[:, :, 0], send_sem.at[0])
    arrived(col_out.at[:, :, 0], send_sem.at[1])
    arrived(row_out.at[0, 0, 0, :224], send_sem.at[2])
    arrived(row_out.at[0, 0, 0, :224], send_sem.at[3])
    for i in range(0, CHUNKS):
        arrived(row_window(i, x, zh, core), row_sent.at[i])
    arrived(view(8, 0), z_sent.at[4])
    for step in range(len(STEPS)):
        sent(step)


def write_kernel(*refs):
    half = len(refs) // 2
    sems = refs[-1]
    pairs = []
    for src, dst in zip(refs[:half], refs[half : 2 * half]):
        if src.shape == dst.shape:
            pairs.append((src, dst))
            continue
        for s in range(16):
            pairs.append((src.at[s // 4, s // 2 % 2, s % 2], dst.at[:, pl.ds(s * COLS, COLS)]))
    copies = [pltpu.make_async_copy(src, dst, sems.at[i]) for i, (src, dst) in enumerate(pairs)]
    for copy in copies:
        copy.start()
    for copy in copies:
        copy.wait()


def body(master, first_moment, second_moment, gradient, step_count):
    block = (ROWS, COLS)
    shapes = [
        (block, F32), (block, F32), (block, F32),
        ((ROWS, 16 * COLS), BF16), ((ROWS, 128), BF16),
        ((4, 2, 2, 16, 16 * ROWS), BF16), ((4, 2, 2, 16, 256), BF16),
    ]
    held_shapes = shapes[:3] + [((4, 2, 2, ROWS, COLS), BF16)] + shapes[4:]
    vmem = pl.BlockSpec(memory_space=pltpu.VMEM)
    hbm = pl.BlockSpec(memory_space=pltpu.HBM)
    dma = pltpu.SemaphoreType.DMA
    place_in = pltpu.with_memory_space_constraint
    held = pl.pallas_call(
        gather_kernel,
        name="gather_copies",
        out_shape=[pltpu.VMEM(shape, dtype) for shape, dtype in held_shapes],
        in_specs=[pl.BlockSpec(memory_space=pltpu.SMEM)] + [hbm] * 4,
        out_specs=[vmem] * 7,
        scratch_shapes=[
            pltpu.VMEM(block, F32), pltpu.VMEM(block, F32), pltpu.VMEM(block, F32), pltpu.VMEM(block, BF16),
            pltpu.VMEM((8, ROWS), F32), pltpu.VMEM((16, COLS), F32), pltpu.VMEM((128, COLS), F32),
            pltpu.VMEM((COLS, ROWS), BF16), pltpu.VMEM((COLS, 128), BF16),
            pltpu.VMEM((4, 16, 4 * ROWS), BF16), pltpu.VMEM((4, 4, 16, 128), BF16),
            pltpu.VMEM((4, 16, 128), BF16), pltpu.VMEM((2, 4, 16, 128), BF16),
            pltpu.VMEM((4, 2, 2, 16, 256), BF16),
            dma((CHUNKS, 4)), dma((10,)), dma((ITEMS,)), dma((ITEMS,)), dma((ITEMS,)), dma((4,)),
            dma((4,)), dma((1,)), dma((1,)), dma((1,)), dma((8,)), dma((1,)),
            dma((WINDOW,)), dma((WINDOW,)), dma((CHUNKS,)), dma((8,)),
        ],
        compiler_params=pltpu.CompilerParams(
            collective_id=0, has_side_effects=True, vmem_limit_bytes=VMEM_LIMIT
        ),
    )(step_count, *(place_in(a, pltpu.HBM) for a in (master, first_moment, second_moment, gradient)))
    new_master, new_first, new_second, row_copy, row_scales, col_copy, col_scales = pl.pallas_call(
        write_kernel,
        name="write_results",
        out_shape=[jax.ShapeDtypeStruct(shape, dtype) for shape, dtype in shapes],
        in_specs=[vmem] * 7,
        out_specs=[hbm] * 7,
        scratch_shapes=[dma((22,))],
        compiler_params=pltpu.CompilerParams(vmem_limit_bytes=VMEM_LIMIT),
    )(*(place_in(a, pltpu.VMEM) for a in held))
    return (
        new_master, new_first, new_second, row_copy, row_scales,
        col_copy.reshape(16, 16, 16 * ROWS), col_scales.reshape(16, 16, 256),
    )


def solution(mesh):
    blocks = P("tp", "shard")
    in_specs = (blocks, blocks, blocks, blocks, P())
    out_specs = (
        blocks, blocks, blocks, P("tp", None), P("tp", None), P(None, "tp", None), P(None, "tp", None),
    )
    return jax.shard_map(body, mesh=mesh, in_specs=in_specs, out_specs=out_specs, check_vma=False)
```

```python
import jax
import jax.numpy as jnp
from jax import lax
from jax.experimental import pallas as pl
from jax.experimental.pallas import tpu as pltpu
from jax.sharding import PartitionSpec as P

beta_one = 0.9
beta_two = 0.95
learn_rate = 0.02
epsilon = 1e-08
floor_value = 0.008
scale_unit = 64.0
block_size = 32

MESH = pl.DeviceIdType.MESH
BF16 = jnp.bfloat16
F32 = jnp.float32

ROWS, COLS, CHUNKS = 512, 256, 4
STEP = ROWS // CHUNKS
VMEM_LIMIT = 24 * 2**20

ROW_SCALES, COL_SCALES, ITEMS = 16, 17, 18

STEPS = (
    (0,), (1,), (2,), (3,), (0, 1), (8,), (2, 3), (4,), (5,), (9,), (15,), (10,), (14,), (8, 5), (11,), (13,),
    (4, 9), (12,), (10, 15), (6,), (7,), (14, 11), (12, 13), (6, 7),
)
WINDOW, ARRIVAL = 3, 4
SMALL = {7: (16,), 13: (17,), 11: (16, None), 17: (None, 17)}
Z_NEAR = (1, 7, 2, 6)
Z_LATER = {6: ((1, 7), (3, 5), ()), 9: ((2, 6), (4,), ()), 12: ((3, 5), (), (2, 3))}
COLUMNS_AT, ROW_SCALES_AT = 5, 20


def place():
    shard, tp = lax.axis_index("shard"), lax.axis_index("tp")
    return shard // 4, (shard // 2) % 2, shard % 2, tp // 4, tp % 4


def device(x, zh, core, zl, y):
    return (x * 4 + zh * 2 + core, zl * 4 + y)


def gather_kernel(
    step_ref, master, first, second, grad,
    new_master, new_first, new_second, row_out, row_scale_out, col_out, cs_out,
    master_v, first_v, second_v, grad_v,
    row_s, col_s, padded, flipped, flipped_s, held, held_s, sums, gathered_s, rs,
    load_sem, send_sem, left_sem, right_sem, opp_sem, sib_sem,
    zrow_sem, zrs_sem, y_sem, ys_sem, z_sem, zs_sem, right_sent, left_sent, row_sent, z_sent,
):
    x, zh, core, zl, y = place()
    z = zh * 4 + zl

    def along(dx=0, dy=0, dz=0, dcore=0):
        zz = (z + dz) % 8
        return device((x + dx) % 4, zz // 4, (core + dcore) % 2, zz % 4, (y + dy) % 4)

    partners = [(0, 0, dz, 0) for dz in (4, 3, 5, 2, 6, 1, 7)]
    partners += [(1, 0, 0, 0), (3, 0, 0, 0), (0, 2, 0, 0), (0, 1, 0, 0), (0, 3, 0, 0), (0, 0, 0, 1)]
    barrier = pltpu.get_barrier_semaphore()
    for partner in partners:
        pl.semaphore_signal(barrier, inc=1, device_id=along(*partner), device_id_type=MESH)

    loads = []
    for i in range(CHUNKS):
        part = pl.ds(i * STEP, STEP)
        loads.append([
            pltpu.make_async_copy(src.at[part], dst.at[part], load_sem.at[i, j])
            for j, (src, dst) in enumerate(
                ((master, master_v), (first, first_v), (second, second_v), (grad, grad_v))
            )
        ])
        for copy in loads[-1]:
            copy.start()

    def row_window(i, xx, half, cc):
        return row_out.at[xx, half, cc, pl.ds(i * STEP, STEP)]

    def view(item, dx):
        xx = (x + dx) % 4
        if item < 4:
            return row_window(item, xx, zh, core)
        if item < 8:
            return row_window(item - 4, xx, 1 - zh, core)
        if item < 16:
            source = (z + 16 - item) % 8
            lanes = pl.multiple_of((source % 4) * 4 * ROWS, 4 * ROWS)
            return col_out.at[xx, source // 4, core, :, pl.ds(lanes, 4 * ROWS)]
        return (rs if item == ROW_SCALES else cs_out).at[xx, :, core]

    def kind(item):
        return 0 if item < 8 else 1 if item < 16 else item - 14

    def remote(src, dst, sent, received, target):
        pltpu.make_async_remote_copy(
            src_ref=src, dst_ref=dst, send_sem=sent, recv_sem=received,
            device_id=target, device_id_type=MESH,
        ).start()

    def arrived(ref, sem):
        pltpu.make_async_copy(ref, ref, sem).wait()

    def move(item, dx, received, target):
        ref = view(item, dx)
        remote(ref, ref, send_sem.at[kind(item)], received, target)

    def to_sibling(item, dx):
        move(item, dx, sib_sem.at[kind(item)], along(dcore=1))

    def row_across(i):
        ref = row_window(i, x, zh, core)
        remote(ref, ref, row_sent.at[i], zrow_sem.at[i], along(dz=4))

    def z_across(dz):
        there = (z + dz) % 8 % 4
        remote(held.at[there], view(8, 0), z_sent.at[dz], z_sem.at[dz], along(dz=dz))

    waited = set()

    def arrive(side, item):
        if (side, item) not in waited:
            waited.add((side, item))
            dx, sem = {"left": (3, left_sem), "right": (1, right_sem), "opposite": (2, opp_sem)}[side]
            arrived(view(item, dx), sem.at[item])
            to_sibling(item, dx)

    def arrivals(group):
        if len(group) == 1:
            arrive("left", group[0])
            arrive("right", group[0])
            return
        for item in group:
            if item is not None:
                arrive("opposite", item)

    def send(group, right_sent, left_sent):
        if len(group) == 1:
            item = group[0]
            at_hand(item)
            ref = view(item, 0)
            remote(ref, ref, right_sent, left_sem.at[item], along(dx=1))
            remote(ref, ref, left_sent, right_sem.at[item], along(dx=3))
            to_sibling(item, 0)
            return
        item, other = group
        if item is not None:
            arrive("left", item)
            remote(view(item, 3), view(item, 3), right_sent, opp_sem.at[item], along(dx=1))
        if other is not None:
            arrive("right", other)
            remote(view(other, 1), view(other, 1), left_sent, opp_sem.at[other], along(dx=3))

    def at_hand(item):
        if 4 <= item < 8:
            arrived(row_window(item - 4, x, 1 - zh, core), zrow_sem.at[item - 4])
        elif 8 <= item < 16:
            arrived(view(item, 0), z_sem.at[item - 8])
        elif item == ROW_SCALES:
            arrived(rs.at[x, 1 - zh, core], zrs_sem.at[0])
        elif item == COL_SCALES:
            arrived(gathered_s, zs_sem.at[0])
            for half in range(2):
                pairs = gathered_s[half].astype(F32)
                low, high = pairs[0] + pairs[1], pairs[2] + pairs[3]
                cs_out[x, half, core] = jnp.concatenate([low, high], axis=1).astype(BF16)

    def sent(step):
        if ("sent", step) not in waited:
            waited.add(("sent", step))
            for sems in (right_sent, left_sent):
                arrived(row_out.at[0, 0, 0, :STEP], sems.at[step % WINDOW])

    def step_out(step):
        if step >= WINDOW:
            sent(step - WINDOW)
        send(STEPS[step], right_sent.at[step % WINDOW], left_sent.at[step % WINDOW])

    steps_done = jnp.full((8, 128), step_ref[0].astype(F32), F32)
    corr_one = (1.0 - jnp.power(beta_one, steps_done))[0:1, 0:1]
    corr_two = (1.0 - jnp.power(beta_two, steps_done))[0:1, 0:1]

    def scale(blocks):
        largest = jnp.max(jnp.abs(blocks), axis=1)
        scales = (scale_unit * jnp.maximum(largest, floor_value)).astype(BF16).astype(F32)
        return scales, blocks * (scale_unit / scales)[:, None, :]

    values = flipped.reshape(4, 4, 16, ROWS)

    def y_across(half):
        here = pl.ds(half * COLS, COLS)
        lanes = pl.ds(pl.multiple_of(y * ROWS + half * COLS, COLS), COLS)
        for dy in (2, 1, 3):
            there = (y + dy) % 4
            remote(values.at[:, there, :, here], held.at[:, :, lanes], send_sem.at[6], y_sem.at[0], along(dy=dy))
        pltpu.make_async_copy(values.at[:, y, :, here], held.at[:, :, lanes], y_sem.at[0]).start()

    for i in range(CHUNKS):
        part = pl.ds(i * STEP, STEP)
        for copy in loads[i]:
            copy.wait()
        g = grad_v[part, :].astype(F32)
        nf = beta_one * first_v[part, :] + (1.0 - beta_one) * g
        nv = beta_two * second_v[part, :] + (1.0 - beta_two) * g * g
        update = nf / corr_one / (jnp.sqrt(nv / corr_two) + epsilon)
        m = master_v[part, :] - learn_rate * update
        new_first[part, :] = nf
        new_second[part, :] = nv
        new_master[part, :] = m

        scales, scaled = scale(m.T.reshape(COLS // block_size, block_size, STEP))
        row_s[:, part] = scales
        row_out[x, zh, core, part, :] = scaled.reshape(COLS, STEP).T.astype(BF16)
        if i == 0:
            pl.semaphore_wait(barrier, len(partners))
        if i < WINDOW:
            step_out(i)
        if i < 2:
            row_across(i)

        scales, scaled = scale(m.reshape(STEP // block_size, block_size, COLS))
        col_s[4 * i : 4 * i + 4, :] = scales
        flipped[:, part] = scaled.reshape(STEP, COLS).T.astype(BF16)
        if i % 2 == 1:
            y_across(i // 2)

    own = row_s[...]
    rs[x, zh, core] = jnp.concatenate([own[:, :COLS], own[:, COLS:]], axis=0).astype(BF16)
    ref = rs.at[x, zh, core]
    remote(ref, ref, send_sem.at[5], zrs_sem.at[0], along(dz=4))

    padded[...] = jnp.zeros_like(padded)
    padded[pl.ds(pl.multiple_of(((zl * 4 + y) % 8) * 16, 16), 16), :] = col_s[...]
    flipped_s[...] = padded[...].T.astype(BF16)
    value_scales = flipped_s.reshape(4, 4, 16, 128)
    for dy in (2, 1, 3):
        there = (y + dy) % 4
        remote(value_scales.at[:, there], held_s.at[y], send_sem.at[7], ys_sem.at[0], along(dy=dy))
    pltpu.make_async_copy(value_scales.at[:, y], held_s.at[y], ys_sem.at[0]).start()

    for step in range(WINDOW, len(STEPS)):
        if step == COLUMNS_AT:
            arrived(held, y_sem.at[0])
            for dz in Z_NEAR:
                z_across(dz)
            pltpu.make_async_copy(held.at[zl], view(8, 0), z_sem.at[0]).start()
        step_out(step)
        if step == COLUMNS_AT:
            arrived(held_s, ys_sem.at[0])
            parts = held_s[...].astype(F32)
            sums[...] = (parts[0] + parts[1] + parts[2] + parts[3]).astype(BF16)
            pltpu.make_async_copy(sums.at[zl], gathered_s.at[zh, zl], zs_sem.at[0]).start()
            for dz in range(1, 8):
                there = (z + dz) % 8 % 4
                remote(sums.at[there], gathered_s.at[zh, zl], send_sem.at[9], zs_sem.at[0], along(dz=dz))
        if step in Z_LATER:
            done, columns, rows = Z_LATER[step]
            for dz in done:
                arrived(view(8, 0), z_sent.at[dz])
            for dz in columns:
                z_across(dz)
            for i in rows:
                row_across(i)
        if step in SMALL:
            group = SMALL[step]
            sems = send_sem.at[max(i or 0 for i in group) - 14]
            send(group, sems, sems)
        if step >= ARRIVAL:
            arrivals(STEPS[step - ARRIVAL])
        if step - ARRIVAL in SMALL:
            arrivals(SMALL[step - ARRIVAL])
        if step == ROW_SCALES_AT + 1:
            arrived(rs.at[:, :, 0], sib_sem.at[2])
            scales = rs[...].astype(F32).reshape(16, 16, COLS)
            for half in range(2):
                one = scales[:, 8 * half : 8 * half + 8].reshape(128, COLS)
                row_scale_out[COLS * half : COLS * (half + 1), :] = one.T.astype(BF16)
    for step in range(len(STEPS) - ARRIVAL, len(STEPS)):
        arrivals(STEPS[step])

    arrived(flipped.at[: 3 * 64], send_sem.at[6])
    arrived(flipped_s.at[: 3 * 64], send_sem.at[7])
    arrived(rs.at[0, 0, 0], send_sem.at[5])
    arrived(row_out.at[0, 0, 0, :112, :128], send_sem.at[9])
    arrived(row_out.at[:, :, 0], send_sem.at[0])
    arrived(col_out.at[:, :, 0], send_sem.at[1])
    arrived(row_out.at[0, 0, 0, :224], send_sem.at[2])
    arrived(row_out.at[0, 0, 0, :224], send_sem.at[3])
    for i in range(0, CHUNKS):
        arrived(row_window(i, x, zh, core), row_sent.at[i])
    arrived(view(8, 0), z_sent.at[4])
    for step in range(len(STEPS)):
        sent(step)
    arrived(cs_out.at[:, :, 0], sib_sem.at[3])
    arrived(row_out.at[:, :, 0], sib_sem.at[0])
    arrived(col_out.at[:, :, 0], sib_sem.at[1])


def write_kernel(*refs):
    half = len(refs) // 2
    sems = refs[-1]
    pairs = []
    for src, dst in zip(refs[:half], refs[half : 2 * half]):
        if src.shape == dst.shape:
            pairs.append((src, dst))
            continue
        for s in range(16):
            pairs.append((src.at[s // 4, s // 2 % 2, s % 2], dst.at[:, pl.ds(s * COLS, COLS)]))
    copies = [pltpu.make_async_copy(src, dst, sems.at[i]) for i, (src, dst) in enumerate(pairs)]
    for copy in copies:
        copy.start()
    for copy in copies:
        copy.wait()


def body(master, first_moment, second_moment, gradient, step_count):
    block = (ROWS, COLS)
    shapes = [
        (block, F32), (block, F32), (block, F32),
        ((ROWS, 16 * COLS), BF16), ((ROWS, 128), BF16),
        ((4, 2, 2, 16, 16 * ROWS), BF16), ((4, 2, 2, 16, 256), BF16),
    ]
    held_shapes = shapes[:3] + [((4, 2, 2, ROWS, COLS), BF16)] + shapes[4:]
    vmem = pl.BlockSpec(memory_space=pltpu.VMEM)
    hbm = pl.BlockSpec(memory_space=pltpu.HBM)
    dma = pltpu.SemaphoreType.DMA
    place_in = pltpu.with_memory_space_constraint
    held = pl.pallas_call(
        gather_kernel,
        name="gather_copies",
        out_shape=[pltpu.VMEM(shape, dtype) for shape, dtype in held_shapes],
        in_specs=[pl.BlockSpec(memory_space=pltpu.SMEM)] + [hbm] * 4,
        out_specs=[vmem] * 7,
        scratch_shapes=[
            pltpu.VMEM(block, F32), pltpu.VMEM(block, F32), pltpu.VMEM(block, F32), pltpu.VMEM(block, BF16),
            pltpu.VMEM((8, ROWS), F32), pltpu.VMEM((16, COLS), F32), pltpu.VMEM((128, COLS), F32),
            pltpu.VMEM((COLS, ROWS), BF16), pltpu.VMEM((COLS, 128), BF16),
            pltpu.VMEM((4, 16, 4 * ROWS), BF16), pltpu.VMEM((4, 4, 16, 128), BF16),
            pltpu.VMEM((4, 16, 128), BF16), pltpu.VMEM((2, 4, 16, 128), BF16),
            pltpu.VMEM((4, 2, 2, 16, 256), BF16),
            dma((CHUNKS, 4)), dma((10,)), dma((ITEMS,)), dma((ITEMS,)), dma((ITEMS,)), dma((4,)),
            dma((4,)), dma((1,)), dma((1,)), dma((1,)), dma((8,)), dma((1,)),
            dma((WINDOW,)), dma((WINDOW,)), dma((CHUNKS,)), dma((8,)),
        ],
        compiler_params=pltpu.CompilerParams(
            collective_id=0, has_side_effects=True, vmem_limit_bytes=VMEM_LIMIT
        ),
    )(step_count, *(place_in(a, pltpu.HBM) for a in (master, first_moment, second_moment, gradient)))
    new_master, new_first, new_second, row_copy, row_scales, col_copy, col_scales = pl.pallas_call(
        write_kernel,
        name="write_results",
        out_shape=[jax.ShapeDtypeStruct(shape, dtype) for shape, dtype in shapes],
        in_specs=[vmem] * 7,
        out_specs=[hbm] * 7,
        scratch_shapes=[dma((22,))],
        compiler_params=pltpu.CompilerParams(vmem_limit_bytes=VMEM_LIMIT),
    )(*(place_in(a, pltpu.VMEM) for a in held))
    return (
        new_master, new_first, new_second, row_copy, row_scales,
        col_copy.reshape(16, 16, 16 * ROWS), col_scales.reshape(16, 16, 256),
    )


def solution(mesh):
    blocks = P("tp", "shard")
    in_specs = (blocks, blocks, blocks, blocks, P())
    out_specs = (
        blocks, blocks, blocks, P("tp", None), P("tp", None), P(None, "tp", None), P(None, "tp", None),
    )
    return jax.shard_map(body, mesh=mesh, in_specs=in_specs, out_specs=out_specs, check_vma=False)
```
